32 devices in a mesh: groups: 2 (over x), tensor: 16 (over z, y, core).
Axes of the slice: x: 2, y: 2, z: 4, core: 2. Of those that a mesh axis runs over, the one named last changes fastest.
Arguments:
- resid: bfloat16 [256, 8192], P(('groups', 'tensor')), parts along dimension 0, may hold values from -100 to 100
- gain: float32 [8192], replicated, may hold values from 0.5 to 1.5
- head: bfloat16 [24000, 8192], P('tensor'), may hold values from -0.176776695 to 0.176776695
- peer: bfloat16 [256, 24000], P('groups', 'tensor'), parts along dimension 0, may hold values from -16 to 260
- labels: int32 [256], P('groups'), parts along dimension 0, may hold values from 0 to 23999
Outputs:
- loss: float32 [2], P('groups'), parts along dimension 0
- input_gradient: bfloat16 [256, 8192], P(('groups', 'tensor')), parts along dimension 0
- head_grad: bfloat16 [48000, 8192], P(('groups', 'tensor')), parts along dimension 0
- gain_gradient: float32 [16384], P('groups'), parts along dimension 0
The draws below stay inside these ranges and needn't reach their ends.
There are 2 independent parts, one for each index of `groups`. The reference program is written for one: setup_inputs(seed, part) draws one part's arguments, and reference() takes and returns one part's arrays. A program takes and returns all parts, laid end to end along the dimension named above; an argument that names none is the same for every part. Nothing has to cross between parts.
All inputs are finite; a program needn't handle non-finite values.
Results may differ from the reference program's by a relative error of at most 0.0055.
Values may be sent and summed in bfloat16 or wider, within the bound.
A program may use at most 128 MiB of HBM per device.

```python
import math
import jax
import jax.numpy as jnp
import numpy as np
from jax import lax

D = 8192
V = 24000
TOKENS = 128


def log_spread(key, shape, low, high):
    return jnp.exp(jax.random.uniform(key, shape, jnp.float32, jnp.log(low), jnp.log(high)))


def draw_resid(key, part):
    key = jax.random.fold_in(key, 3)
    keys = jax.random.split(key, 3)
    row_scale = log_spread(keys[0], (TOKENS, 1), 0.5, 5.0)
    col_scale = log_spread(keys[1], (1, D), 0.5, 5.0)
    base = jnp.clip(jax.random.normal(keys[2], (TOKENS, D), jnp.float32), -4.0, 4.0)
    values = base * row_scale * col_scale
    return values.astype(jnp.bfloat16)


def draw_head(key, part):
    key = jax.random.fold_in(key, 5)
    keys = jax.random.split(key, 2)
    position = jnp.arange(V, dtype=jnp.float32)[:, None]
    sigma = (3.0 + 0.4 * position / (V - 1)) * log_spread(keys[0], (V, 1), 0.97, 1.03) / jnp.sqrt(float(D))
    values = jnp.clip(jax.random.normal(keys[1], (V, D), jnp.float32), -4.0, 4.0) * sigma
    return values.astype(jnp.bfloat16)


def draw_peer(key, part):
    key = jax.random.fold_in(key, 7)
    keys = jax.random.split(key, 1)
    sigma = (3.0 + 0.4 * jnp.arange(V, dtype=jnp.float32) / (V - 1))[None, :]
    values = jnp.clip(jax.random.normal(keys[0], (TOKENS, V), jnp.float32), -4.0, 4.0) * sigma
    return values.astype(jnp.bfloat16)


def touch_ends(entries, rng, low, top_value):
    place = [jax.random.randint(jax.random.fold_in(rng, axis), (), 0, length) for axis, length in enumerate(entries.shape)]
    main_axis = entries.shape.index(max(entries.shape))
    neighbour = place[:main_axis] + [(place[main_axis] + 1) % entries.shape[main_axis]] + place[main_axis + 1:]
    return entries.at[tuple(place)].set(low).at[tuple(neighbour)].set(top_value)


def rank_table(number_of, skew):
    loads = [(1 << 20) // math.isqrt(rank ** skew) + 1 for rank in range(1, number_of + 1)]
    spread = 1 + sum(loads) // (1 << 30)
    return np.cumsum(np.array([max(1, weight // spread) for weight in loads]))


def skewed_ids(own_key, shape, count, skew):
    listing = rank_table(count, skew)
    lot = jax.random.randint(jax.random.fold_in(own_key, 1), shape, 0, int(listing[count - 1]))
    grade = jnp.searchsorted(jnp.asarray(listing, jnp.int32), lot, side="right")
    return jax.random.permutation(jax.random.fold_in(own_key, 2), count)[grade].astype(jnp.int32)


def setup_inputs(seed: int = 0, part: int = 0) -> dict:
    streams_of = jax.random.split(jax.random.key(seed), 6)
    part_splits = jax.random.split(jax.random.fold_in(streams_of[5], part), 6)
    return {
        "resid": draw_resid(jax.random.fold_in(jax.random.fold_in(streams_of[5], part), 71), part),
        "gain": jnp.clip(1.0 + 0.1 * jax.random.normal(streams_of[1], (D,), jnp.float32), 0.5, 1.5),
        "head": draw_head(jax.random.fold_in(streams_of[5], 71), part),
        "peer": draw_peer(jax.random.fold_in(jax.random.fold_in(streams_of[5], part), 71), part),
        "labels": touch_ends(skewed_ids(part_splits[4], (TOKENS,), V, 2), jax.random.fold_in(part_splits[4], 3), 0, V - 1).astype(jnp.int32),
    }


BETA = 0.5
EPS = 1e-05

def reference(resid, gain, head, peer, labels):
    widened_rows = resid.astype(jnp.float32)
    inverse_scale = lax.rsqrt(lax.optimization_barrier(jnp.mean(widened_rows * widened_rows, axis=1, keepdims=True)) + EPS)
    centered_input = widened_rows * inverse_scale
    scaled_rows = (centered_input * gain).astype(jnp.bfloat16)
    logits = jnp.dot(scaled_rows, head.T, preferred_element_type=jnp.float32)
    smax = lax.optimization_barrier(jnp.max(logits, axis=1, keepdims=True))
    student_exp = jnp.exp(logits - smax)
    ssum = lax.optimization_barrier(jnp.sum(student_exp, axis=1, keepdims=True))
    other = peer.astype(jnp.float32)
    pmax = lax.optimization_barrier(jnp.max(other, axis=1, keepdims=True))
    peer_exp = jnp.exp(other - pmax)
    partial_sum = lax.optimization_barrier(jnp.sum(peer_exp, axis=1, keepdims=True))
    cross = lax.optimization_barrier(jnp.sum(peer_exp * (other - logits), axis=1, keepdims=True)) / partial_sum
    column = jnp.arange(V, dtype=jnp.int32)[None, :]
    match = column == labels.astype(jnp.int32)[:, None]
    label_logit = lax.optimization_barrier(jnp.sum(jnp.where(match, logits, 0.0), axis=1, keepdims=True))
    student_lse = smax + jnp.log(ssum)
    peer_lse = pmax + jnp.log(partial_sum)
    per_token = student_lse - label_logit + BETA * (cross - peer_lse + student_lse)
    loss = jnp.mean(per_token).reshape(1)
    student_prob = student_exp / ssum
    peer_prob = peer_exp / partial_sum
    dlogits = ((1.0 + BETA) * student_prob - match.astype(jnp.float32) - BETA * peer_prob).astype(jnp.bfloat16)
    head_grad = jnp.dot(dlogits.T, scaled_rows, preferred_element_type=jnp.float32).astype(jnp.bfloat16)
    normalized_grad = jnp.dot(dlogits, head, preferred_element_type=jnp.float32)
    gain_gradient = lax.optimization_barrier(jnp.sum(normalized_grad * centered_input, axis=0))
    gain_weighted = gain * normalized_grad
    input_gradient = (inverse_scale * gain_weighted - centered_input * inverse_scale * lax.optimization_barrier(jnp.mean(gain_weighted * centered_input, axis=1, keepdims=True))).astype(jnp.bfloat16)
    return (loss, input_gradient, head_grad, gain_gradient)
```

```python
import functools

import jax
import jax.numpy as jnp
from jax import lax
from jax.experimental import pallas as pl
from jax.experimental.pallas import tpu as pltpu
from jax.sharding import PartitionSpec as P

BETA = 0.5
EPS = 1e-05
PARTS = 4
CHUNK = 512
VMEM_BYTES = 58 * 1024 * 1024


def remote(src, dst, send, recv, device):
    return pltpu.make_async_remote_copy(
        src_ref=src,
        dst_ref=dst,
        send_sem=send,
        recv_sem=recv,
        device_id={"tensor": device},
        device_id_type=pl.DeviceIdType.MESH,
    )


def head_kernel(
    n,
    resid_ref,
    gain_ref,
    head_ref,
    peer_ref,
    labels_ref,
    loss_ref,
    input_grad_ref,
    gain_grad_ref,
    dlogits_ref,
    normed_out,
    hbuf,
    normed,
    xhat,
    xswap,
    xchip,
    logits,
    other,
    stat,
    dl,
    acc,
    sib_out,
    sib_in,
    y_out,
    y_in,
    z_out,
    z_in,
    own,
    dnfull,
    gparts,
    gfull,
    head_sem,
    swap_sem,
    az_send,
    ay_send,
    ab_send,
    ac_recv,
    ab_recv,
    st_send,
    st_recv,
    sib_sem,
    y_sem,
    z_send,
    z_recv,
    f_send,
    f_recv,
    g_send,
    g_recv,
    h_sem,
    out_sem,
):
    nk, vocab, bk = hbuf.shape
    _, tokens, half = normed.shape
    rows = resid_ref.shape[0]
    pair = 2 * rows
    w = half // PARTS
    sub = w // bk
    nz = n // 4
    chips = n // 2

    me = lax.axis_index("tensor")
    c = me % 2
    y = (me // 2) % 2
    z = me // 4
    chip = z * 2 + y
    sibling = chip * 2 + (1 - c)
    across = (z * 2 + (1 - y)) * 2 + c

    def head_copy(k):
        return pltpu.make_async_copy(
            head_ref.at[:, pl.ds(k * bk, bk)], hbuf.at[k], head_sem.at[k]
        )

    barrier = pltpu.get_barrier_semaphore()

    def greet(d, carry):
        pl.semaphore_signal(
            barrier, inc=1, device_id={"tensor": (me + d) % n}, device_id_type=pl.DeviceIdType.MESH
        )
        return carry

    lax.fori_loop(1, n, greet, 0)

    for p in range(PARTS):
        for h in range(2):
            for s in range(sub):
                head_copy(h * (nk // 2) + p * sub + s).start()

    wide = resid_ref[...].astype(jnp.float32)
    scale = lax.rsqrt(jnp.mean(wide * wide, axis=1, keepdims=True) + EPS)
    for h in range(2):
        xhat[h] = wide[:, h * half : (h + 1) * half] * scale

    pl.semaphore_wait(barrier, n - 1)

    swap = remote(xhat.at[1 - c], xswap, swap_sem.at[0], swap_sem.at[1], sibling)
    swap.start()
    swap.wait()
    mine = xhat[c]
    theirs = xswap[...]
    first = c == 0
    xchip[pl.ds(0, rows), :] = jnp.where(first, mine, theirs)
    xchip[pl.ds(rows, rows), :] = jnp.where(first, theirs, mine)
    normed[c, pl.ds(pl.multiple_of(chip * pair, 16), pair), :] = (
        xchip[...] * gain_ref[c]
    ).astype(jnp.bfloat16)

    def block(chip_i, p):
        return normed.at[c, pl.ds(pl.multiple_of(chip_i * pair, 16), pair), pl.ds(p * w, w)]

    def block_b(chip_i, p):
        return normed.at[1 - c, pl.ds(pl.multiple_of(chip_i * pair, 16), pair), pl.ds(p * w, w)]

    def along(d):
        return (z + d) % nz

    def to_z(p, d):
        b = block(chip, p)
        return remote(
            b, b, az_send.at[p, d], ac_recv.at[p, chip], (along(d) * 2 + y) * 2 + c
        )

    def to_y(p, d):
        j = along(d) * 2 + y
        b = block(j, p)
        return remote(b, b, ay_send.at[p, d], ac_recv.at[p, j], across)

    def to_sibling(p, j):
        b = block(j, p)
        return remote(b, b, ab_send.at[p, j], ab_recv.at[p, j], sibling)

    def arrived(p, j):
        b = block(j, p)
        remote(b, b, ay_send.at[p, 0], ac_recv.at[p, j], across).wait_recv()

    def arrived_b(p, j):
        b = block_b(j, p)
        remote(b, b, ab_send.at[p, j], ab_recv.at[p, j], sibling).wait_recv()

    for p in range(PARTS):
        to_y(p, 0).start()
        for d in range(1, nz):
            to_z(p, d).start()
        to_sibling(p, chip).start()

    other[...] = jnp.transpose(peer_ref[...].astype(jnp.float32))
    ptop = jnp.max(other[...], axis=0, keepdims=True)
    psum = jnp.sum(jnp.exp(other[...] - ptop), axis=0, keepdims=True)
    stat[me, 2:3, :] = ptop
    stat[me, 3:4, :] = psum
    logits[...] = jnp.zeros_like(logits)

    def add_logits(p):
        def step(i, carry):
            h = i // sub
            at = p * sub + i % sub
            k = h * (nk // 2) + at
            x = normed[h, :, pl.ds(pl.multiple_of(at * bk, bk), bk)]
            logits[...] += lax.dot_general(
                hbuf[k], x, (((1,), (1,)), ((), ())), preferred_element_type=jnp.float32
            )
            return carry

        lax.fori_loop(0, 2 * sub, step, 0)

    for i in range(PARTS + 2):
        if i < PARTS:
            for d in range(1, nz):
                j = along(d) * 2 + y
                arrived(i, j)
                to_y(i, d).start()
                to_sibling(i, j).start()
        if 0 <= i - 1 < PARTS:
            for d in range(nz):
                j = along(d) * 2 + (1 - y)
                arrived(i - 1, j)
                to_sibling(i - 1, j).start()
        if 0 <= i - 2 < PARTS:
            p = i - 2
            for j in range(chips):
                arrived_b(p, j)
            for h in range(2):
                for s in range(sub):
                    head_copy(h * (nk // 2) + p * sub + s).wait()
            add_logits(p)

    out_normed = pltpu.make_async_copy(normed, normed_out, out_sem.at[0])
    out_normed.start()

    column = me * vocab + lax.broadcasted_iota(jnp.int32, (vocab, tokens), 0)
    match = column == labels_ref[...]
    top = jnp.max(logits[...], axis=0, keepdims=True)
    stat[me, 0:1, :] = top
    stat[me, 1:2, :] = jnp.sum(jnp.exp(logits[...] - top), axis=0, keepdims=True)
    stat[me, 4:5, :] = jnp.sum(
        jnp.exp(other[...] - ptop) * (other[...] - logits[...]), axis=0, keepdims=True
    )
    stat[me, 5:6, :] = jnp.sum(jnp.where(match, logits[...], 0.0), axis=0, keepdims=True)
    stat[me, 6:8, :] = jnp.zeros((2, tokens), jnp.float32)

    def stat_copy(d):
        return remote(
            stat.at[me], stat.at[me], st_send.at[d], st_recv.at[me], (me + d) % n
        )

    def send_stat(d, carry):
        stat_copy(d).start()
        return carry

    def wait_stat(d, carry):
        j = (me + d) % n
        remote(stat.at[j], stat.at[j], st_send.at[d], st_recv.at[j], j).wait_recv()
        return carry

    lax.fori_loop(1, n, send_stat, 0)
    lax.fori_loop(1, n, wait_stat, 0)

    top_all = stat[0, 0:1, :]
    ptop_all = stat[0, 2:3, :]
    for j in range(1, n):
        top_all = jnp.maximum(top_all, stat[j, 0:1, :])
        ptop_all = jnp.maximum(ptop_all, stat[j, 2:3, :])
    sum_s = jnp.zeros_like(top_all)
    sum_p = jnp.zeros_like(top_all)
    cross = jnp.zeros_like(top_all)
    label_logit = jnp.zeros_like(top_all)
    for j in range(n):
        sum_s += stat[j, 1:2, :] * jnp.exp(stat[j, 0:1, :] - top_all)
        weight = jnp.exp(stat[j, 2:3, :] - ptop_all)
        sum_p += stat[j, 3:4, :] * weight
        cross += stat[j, 4:5, :] * weight
        label_logit += stat[j, 5:6, :]
    student_lse = top_all + jnp.log(sum_s)
    peer_lse = ptop_all + jnp.log(sum_p)
    per_token = student_lse - label_logit + BETA * (cross / sum_p - peer_lse + student_lse)
    loss_ref[...] = jnp.mean(per_token, axis=1, keepdims=True)

    grad = (
        (1.0 + BETA) / sum_s * jnp.exp(logits[...] - top_all)
        - match.astype(jnp.float32)
        - BETA / sum_p * jnp.exp(other[...] - ptop_all)
    )
    dlogits_ref[...] = grad.astype(jnp.bfloat16)
    dl[...] = jnp.transpose(grad).astype(jnp.bfloat16)

    def product(h, at):
        return jnp.dot(dl[...], hbuf[h * (nk // 2) + at], preferred_element_type=jnp.float32)

    def sib_copy(p):
        return remote(sib_out.at[p], sib_in.at[p], sib_sem.at[0, p], sib_sem.at[1, p], sibling)

    def y_copy(p):
        return remote(y_out.at[p], y_in.at[p], y_sem.at[0, p], y_sem.at[1, p], across)

    def z_copy(p, d):
        return remote(
            z_out.at[p, d],
            z_in.at[p, d],
            z_send.at[p, d],
            z_recv.at[p, d],
            (along(d) * 2 + y) * 2 + c,
        )

    def f_copy(p):
        return remote(
            own.at[p, pl.ds(pl.multiple_of((1 - c) * rows, 8), rows), :],
            dnfull.at[c, :, pl.ds(p * w, w)],
            f_send.at[p],
            f_recv.at[p],
            sibling,
        )

    def f_arrival(p):
        return remote(
            dnfull.at[1 - c, :, pl.ds(p * w, w)],
            dnfull.at[1 - c, :, pl.ds(p * w, w)],
            f_send.at[p],
            f_recv.at[p],
            sibling,
        )

    for i in range(PARTS + 3):
        if i < PARTS:

            def other_half(s, carry, i=i):
                sib_out[i, :, pl.ds(pl.multiple_of(s * bk, bk), bk)] = product(
                    1 - c, i * sub + s
                ).astype(jnp.bfloat16)
                return carry

            def own_half(s, carry, i=i):
                acc[i, :, pl.ds(pl.multiple_of(s * bk, bk), bk)] = product(c, i * sub + s)
                return carry

            lax.fori_loop(0, sub, other_half, 0)
            sib_copy(i).start()
            lax.fori_loop(0, sub, own_half, 0)
        if 0 <= i - 1 < PARTS:
            p = i - 1
            sib_copy(p).wait_recv()
            for d in range(nz):
                at = pl.ds(pl.multiple_of((d * 2 + 1 - y) * pair, 16), pair)
                y_out[p, d] = (acc[p, at, :] + sib_in[p, at, :].astype(jnp.float32)).astype(
                    jnp.bfloat16
                )
            y_copy(p).start()
        if 0 <= i - 2 < PARTS:
            p = i - 2
            y_copy(p).wait_recv()
            for d in range(nz):
                to = along(d)
                at = pl.ds(pl.multiple_of((to * 2 + y) * pair, 16), pair)
                total = (
                    acc[p, at, :]
                    + sib_in[p, at, :].astype(jnp.float32)
                    + y_in[p, to].astype(jnp.float32)
                )
                if d == 0:
                    own[p] = total
                else:
                    z_out[p, d] = total.astype(jnp.bfloat16)
                    z_copy(p, d).start()
        if 0 <= i - 3 < PARTS:
            p = i - 3
            total = own[p]
            for d in range(1, nz):
                z_copy(p, d).wait_recv()
                total += z_in[p, d].astype(jnp.float32)
            own[p] = total
            f_copy(p).start()
            dnfull[c, :, pl.ds(p * w, w)] = own[p, pl.ds(pl.multiple_of(c * rows, 8), rows), :]
            gparts[chip, :, pl.ds(p * w, w)] = jnp.sum(
                total * xchip[:, pl.ds(p * w, w)], axis=0, keepdims=True
            )

    def g_copy(d):
        to = (chip + d) % chips
        return remote(
            gparts.at[chip], gparts.at[chip], g_send.at[d], g_recv.at[chip], to * 2 + c
        )

    def send_g(d, carry):
        g_copy(d).start()
        return carry

    def wait_g(d, carry):
        j = (chip + d) % chips
        remote(gparts.at[j], gparts.at[j], g_send.at[d], g_recv.at[j], sibling).wait_recv()
        return carry

    lax.fori_loop(1, chips, send_g, 0)

    for p in range(PARTS):
        f_arrival(p).wait_recv()
    mean = jnp.zeros((rows, 1), jnp.float32)
    for h in range(2):
        mean += jnp.sum(gain_ref[h] * dnfull[h] * xhat[h], axis=1, keepdims=True)
    mean = mean / (2 * half)
    for h in range(2):
        input_grad_ref[:, h * half : (h + 1) * half] = (
            scale * (gain_ref[h] * dnfull[h]) - xhat[h] * scale * mean
        ).astype(jnp.bfloat16)

    lax.fori_loop(1, chips, wait_g, 0)
    total = gparts[0]
    for j in range(1, chips):
        total += gparts[j]
    gfull[c] = total
    last = remote(gfull.at[c], gfull.at[c], h_sem.at[0], h_sem.at[1], sibling)
    last.start()
    last.wait_send()
    remote(gfull.at[1 - c], gfull.at[1 - c], h_sem.at[0], h_sem.at[1], sibling).wait_recv()
    gain_grad_ref[...] = gfull[...]

    for p in range(PARTS):
        for d in range(nz):
            to_y(p, d).wait_send()
            if d:
                to_z(p, d).wait_send()
                z_copy(p, d).wait_send()
        for j in range(chips):
            to_sibling(p, j).wait_send()
        sib_copy(p).wait_send()
        y_copy(p).wait_send()
        f_copy(p).wait_send()

    def drain_stat(d, carry):
        stat_copy(d).wait_send()
        return carry

    def drain_g(d, carry):
        g_copy(d).wait_send()
        return carry

    lax.fori_loop(1, n, drain_stat, 0)
    lax.fori_loop(1, chips, drain_g, 0)
    out_normed.wait()


def head_grad_kernel(dlogits_ref, normed_ref, out_ref):
    out_ref[...] = jnp.dot(
        dlogits_ref[...], normed_ref[...], preferred_element_type=jnp.float32
    ).astype(jnp.bfloat16)


def per_device(n, resid, gain, head, peer, labels):
    rows, depth = resid.shape
    tokens, vocab = peer.shape
    half = depth // 2
    w = half // PARTS
    bk = min(CHUNK, w)
    nk = depth // bk
    nz = n // 4
    chips = n // 2
    pair = 2 * rows
    f32, bf16 = jnp.float32, jnp.bfloat16
    dma = pltpu.SemaphoreType.DMA
    vmem = pl.BlockSpec(memory_space=pltpu.VMEM)
    hbm = pl.BlockSpec(memory_space=pl.ANY)
    loss, input_grad, gain_grad, dlogits, normed = pl.pallas_call(
        functools.partial(head_kernel, n),
        out_shape=(
            jax.ShapeDtypeStruct((1, 1), f32),
            jax.ShapeDtypeStruct((rows, depth), bf16),
            jax.ShapeDtypeStruct((2, 1, half), f32),
            jax.ShapeDtypeStruct((vocab, tokens), bf16),
            jax.ShapeDtypeStruct((2, tokens, half), bf16),
        ),
        in_specs=[vmem, vmem, hbm, vmem, vmem],
        out_specs=(vmem, vmem, vmem, vmem, hbm),
        scratch_shapes=[
            pltpu.VMEM((nk, vocab, bk), bf16),
            pltpu.VMEM((2, tokens, half), bf16),
            pltpu.VMEM((2, rows, half), f32),
            pltpu.VMEM((rows, half), f32),
            pltpu.VMEM((pair, half), f32),
            pltpu.VMEM((vocab, tokens), f32),
            pltpu.VMEM((vocab, tokens), f32),
            pltpu.VMEM((n, 8, tokens), f32),
            pltpu.VMEM((tokens, vocab), bf16),
            pltpu.VMEM((PARTS, tokens, w), f32),
            pltpu.VMEM((PARTS, tokens, w), bf16),
            pltpu.VMEM((PARTS, tokens, w), bf16),
            pltpu.VMEM((PARTS, nz, pair, w), bf16),
            pltpu.VMEM((PARTS, nz, pair, w), bf16),
            pltpu.VMEM((PARTS, nz, pair, w), bf16),
            pltpu.VMEM((PARTS, nz, pair, w), bf16),
            pltpu.VMEM((PARTS, pair, w), f32),
            pltpu.VMEM((2, rows, half), f32),
            pltpu.VMEM((chips, 1, half), f32),
            pltpu.VMEM((2, 1, half), f32),
            dma((nk,)),
            dma((2,)),
            dma((PARTS, nz)),
            dma((PARTS, nz)),
            dma((PARTS, chips)),
            dma((PARTS, chips)),
            dma((PARTS, chips)),
            dma((n,)),
            dma((n,)),
            dma((2, PARTS)),
            dma((2, PARTS)),
            dma((PARTS, nz)),
            dma((PARTS, nz)),
            dma((PARTS,)),
            dma((PARTS,)),
            dma((chips,)),
            dma((chips,)),
            dma((2,)),
            dma((1,)),
        ],
        compiler_params=pltpu.CompilerParams(
            collective_id=0, has_side_effects=True, vmem_limit_bytes=VMEM_BYTES
        ),
        cost_estimate=pl.CostEstimate(
            flops=4 * tokens * vocab * depth,
            bytes_accessed=2 * vocab * depth,
            transcendentals=4 * tokens * vocab,
        ),
    )(resid, gain.reshape(2, 1, half), head, peer, labels.reshape(1, tokens))

    per_half = half // bk
    head_grad = pl.pallas_call(
        head_grad_kernel,
        grid=(nk,),
        out_shape=jax.ShapeDtypeStruct((vocab, depth), bf16),
        in_specs=[
            pl.BlockSpec((vocab, tokens), lambda k: (0, 0)),
            pl.BlockSpec((None, tokens, bk), lambda k: (k // per_half, 0, k % per_half)),
        ],
        out_specs=pl.BlockSpec((vocab, bk), lambda k: (0, k)),
        compiler_params=pltpu.CompilerParams(vmem_limit_bytes=VMEM_BYTES),
        cost_estimate=pl.CostEstimate(
            flops=2 * tokens * vocab * depth,
            bytes_accessed=2 * vocab * depth,
            transcendentals=0,
        ),
    )(dlogits, normed)
    return loss.reshape(1), input_grad, head_grad, gain_grad.reshape(depth)


def solution(mesh):
    return jax.shard_map(
        functools.partial(per_device, mesh.shape["tensor"]),
        mesh=mesh,
        in_specs=(
            P(("groups", "tensor"), None),
            P(),
            P("tensor", None),
            P("groups", "tensor"),
            P("groups"),
        ),
        out_specs=(
            P("groups"),
            P(("groups", "tensor"), None),
            P(("groups", "tensor"), None),
            P("groups"),
        ),
        check_vma=False,
    )
```

```python
import functools

import jax
import jax.numpy as jnp
from jax import lax
from jax.experimental import pallas as pl
from jax.experimental.pallas import tpu as pltpu
from jax.sharding import PartitionSpec as P

BETA = 0.5
EPS = 1e-05
PARTS = 4
CHUNK = 512
GROUPED = 1
OUT_COLUMNS = 1024
VMEM_BYTES = 58 * 1024 * 1024


def remote(src, dst, send, recv, device):
    return pltpu.make_async_remote_copy(
        src_ref=src,
        dst_ref=dst,
        send_sem=send,
        recv_sem=recv,
        device_id={"tensor": device},
        device_id_type=pl.DeviceIdType.MESH,
    )


def head_kernel(
    n,
    resid_ref,
    gain_ref,
    head_ref,
    peer_ref,
    labels_ref,
    loss_ref,
    input_grad_ref,
    gain_grad_ref,
    dlogits_ref,
    normed_out,
    hbuf,
    normed,
    xhat,
    xswap,
    xchip,
    logits,
    other,
    student_exp,
    peer_exp,
    stat,
    dl,
    acc,
    sib_out,
    sib_in,
    y_out,
    y_in,
    z_out,
    z_in,
    own,
    dnfull,
    gparts,
    gfull,
    head_sem,
    swap_sem,
    az_send,
    ay_send,
    ab_send,
    ac_recv,
    ab_recv,
    st_send,
    st_recv,
    sib_sem,
    y_sem,
    z_send,
    z_recv,
    f_send,
    f_recv,
    g_send,
    g_recv,
    h_sem,
    out_sem,
):
    nk, vocab, bk = hbuf.shape
    _, tokens, half = normed.shape
    rows = resid_ref.shape[0]
    pair = 2 * rows
    w = half // PARTS
    sub = w // bk
    nz = n // 4
    chips = n // 2

    me = lax.axis_index("tensor")
    c = me % 2
    y = (me // 2) % 2
    z = me // 4
    chip = z * 2 + y
    sibling = chip * 2 + (1 - c)
    across = (z * 2 + (1 - y)) * 2 + c

    def head_copy(k):
        return pltpu.make_async_copy(
            head_ref.at[:, pl.ds(k * bk, bk)], hbuf.at[k], head_sem.at[k]
        )

    barrier = pltpu.get_barrier_semaphore()

    def greet(d, carry):
        pl.semaphore_signal(
            barrier, inc=1, device_id={"tensor": (me + d) % n}, device_id_type=pl.DeviceIdType.MESH
        )
        return carry

    lax.fori_loop(1, n, greet, 0)

    for p in range(PARTS):
        for h in range(2):
            for s in range(sub):
                head_copy(h * (nk // 2) + p * sub + s).start()

    wide = resid_ref[...].astype(jnp.float32)
    scale = lax.rsqrt(jnp.mean(wide * wide, axis=1, keepdims=True) + EPS)
    for h in range(2):
        xhat[h] = wide[:, h * half : (h + 1) * half] * scale

    pl.semaphore_wait(barrier, n - 1)

    swap = remote(xhat.at[1 - c], xswap, swap_sem.at[0], swap_sem.at[1], sibling)
    swap.start()
    swap.wait()
    mine = xhat[c]
    theirs = xswap[...]
    first = c == 0
    xchip[pl.ds(0, rows), :] = jnp.where(first, mine, theirs)
    xchip[pl.ds(rows, rows), :] = jnp.where(first, theirs, mine)
    normed[c, pl.ds(pl.multiple_of(chip * pair, 16), pair), :] = (
        xchip[...] * gain_ref[c]
    ).astype(jnp.bfloat16)

    def block(chip_i, p):
        return normed.at[c, pl.ds(pl.multiple_of(chip_i * pair, 16), pair), pl.ds(p * w, w)]

    def block_b(chip_i, p):
        return normed.at[1 - c, pl.ds(pl.multiple_of(chip_i * pair, 16), pair), pl.ds(p * w, w)]

    def along(d):
        return (z + d) % nz

    def to_z(p, d):
        b = block(chip, p)
        return remote(
            b, b, az_send.at[p, d], ac_recv.at[p, chip], (along(d) * 2 + y) * 2 + c
        )

    def to_y(p, d):
        j = along(d) * 2 + y
        b = block(j, p)
        return remote(b, b, ay_send.at[p, d], ac_recv.at[p, j], across)

    def to_sibling(p, j):
        b = block(j, p)
        return remote(b, b, ab_send.at[p, j], ab_recv.at[p, j], sibling)

    def arrived(p, j):
        b = block(j, p)
        remote(b, b, ay_send.at[p, 0], ac_recv.at[p, j], across).wait_recv()

    def arrived_b(p, j):
        b = block_b(j, p)
        remote(b, b, ab_send.at[p, j], ab_recv.at[p, j], sibling).wait_recv()

    for p in range(PARTS):
        to_y(p, 0).start()
        for d in range(1, nz):
            to_z(p, d).start()
        to_sibling(p, chip).start()

    other[...] = peer_ref[...].astype(jnp.float32)
    ptop = jnp.max(other[...], axis=0, keepdims=True)
    peer_exp[...] = jnp.exp(other[...] - ptop)
    psum = jnp.sum(peer_exp[...], axis=0, keepdims=True)
    stat[me, 2:3, :] = ptop
    stat[me, 3:4, :] = psum
    logits[...] = jnp.zeros_like(logits)

    def add_logits(p):
        def step(i, carry):
            h = i // sub
            at = p * sub + i % sub
            k = h * (nk // 2) + at
            x = normed[h, :, pl.ds(pl.multiple_of(at * bk, bk), bk)]
            logits[...] += lax.dot_general(
                hbuf[k], x, (((1,), (1,)), ((), ())), preferred_element_type=jnp.float32
            )
            return carry

        lax.fori_loop(0, 2 * sub, step, 0)

    for i in range(PARTS + 2):
        if i < PARTS:
            for d in range(1, nz):
                j = along(d) * 2 + y
                arrived(i, j)
                to_y(i, d).start()
                to_sibling(i, j).start()
        if 0 <= i - 1 < PARTS:
            for d in range(nz):
                j = along(d) * 2 + (1 - y)
                arrived(i - 1, j)
                to_sibling(i - 1, j).start()
        if 0 <= i - 2 < PARTS:
            p = i - 2
            for j in range(chips):
                arrived_b(p, j)
            for h in range(2):
                for s in range(sub):
                    head_copy(h * (nk // 2) + p * sub + s).wait()
            add_logits(p)

    out_normed = pltpu.make_async_copy(normed, normed_out, out_sem.at[0])
    out_normed.start()

    column = me * vocab + lax.broadcasted_iota(jnp.int32, (vocab, tokens), 0)
    match = column == labels_ref[...]
    top = jnp.max(logits[...], axis=0, keepdims=True)
    stat[me, 0:1, :] = top
    student_exp[...] = jnp.exp(logits[...] - top)
    stat[me, 1:2, :] = jnp.sum(student_exp[...], axis=0, keepdims=True)
    stat[me, 4:5, :] = jnp.sum(
        peer_exp[...] * (other[...] - logits[...]), axis=0, keepdims=True
    )
    stat[me, 5:6, :] = jnp.sum(jnp.where(match, logits[...], 0.0), axis=0, keepdims=True)
    stat[me, 6:8, :] = jnp.zeros((2, tokens), jnp.float32)

    def stat_copy(d):
        return remote(
            stat.at[me], stat.at[me], st_send.at[d], st_recv.at[me], (me + d) % n
        )

    def send_stat(d, carry):
        stat_copy(d).start()
        return carry

    def wait_stat(d, carry):
        j = (me + d) % n
        remote(stat.at[j], stat.at[j], st_send.at[d], st_recv.at[j], j).wait_recv()
        return carry

    lax.fori_loop(1, n, send_stat, 0)
    lax.fori_loop(1, n, wait_stat, 0)

    top_all = stat[0, 0:1, :]
    ptop_all = stat[0, 2:3, :]
    for j in range(1, n):
        top_all = jnp.maximum(top_all, stat[j, 0:1, :])
        ptop_all = jnp.maximum(ptop_all, stat[j, 2:3, :])
    sum_s = jnp.zeros_like(top_all)
    sum_p = jnp.zeros_like(top_all)
    cross = jnp.zeros_like(top_all)
    label_logit = jnp.zeros_like(top_all)
    for j in range(n):
        sum_s += stat[j, 1:2, :] * jnp.exp(stat[j, 0:1, :] - top_all)
        weight = jnp.exp(stat[j, 2:3, :] - ptop_all)
        sum_p += stat[j, 3:4, :] * weight
        cross += stat[j, 4:5, :] * weight
        label_logit += stat[j, 5:6, :]
    student_lse = top_all + jnp.log(sum_s)
    peer_lse = ptop_all + jnp.log(sum_p)
    per_token = student_lse - label_logit + BETA * (cross / sum_p - peer_lse + student_lse)
    loss_ref[...] = jnp.mean(per_token, axis=1, keepdims=True)

    grad = (
        (1.0 + BETA) * jnp.exp(top - top_all) / sum_s * student_exp[...]
        - match.astype(jnp.float32)
        - BETA * jnp.exp(ptop - ptop_all) / sum_p * peer_exp[...]
    )
    dlogits_ref[...] = grad.astype(jnp.bfloat16)
    dl[...] = jnp.transpose(grad).astype(jnp.bfloat16)

    def product(h, at):
        return jnp.dot(dl[...], hbuf[h * (nk // 2) + at], preferred_element_type=jnp.float32)

    def sib_copy(p):
        return remote(sib_out.at[p], sib_in.at[p], sib_sem.at[0, p], sib_sem.at[1, p], sibling)

    def y_copy(p):
        return remote(y_out.at[p], y_in.at[p], y_sem.at[0, p], y_sem.at[1, p], across)

    def z_copy(p, d):
        return remote(
            z_out.at[p, d],
            z_in.at[p, d],
            z_send.at[p, d],
            z_recv.at[p, d],
            (along(d) * 2 + y) * 2 + c,
        )

    def f_copy(p):
        return remote(
            own.at[p, pl.ds(pl.multiple_of((1 - c) * rows, 8), rows), :],
            dnfull.at[c, :, pl.ds(p * w, w)],
            f_send.at[p],
            f_recv.at[p],
            sibling,
        )

    def f_arrival(p):
        return remote(
            dnfull.at[1 - c, :, pl.ds(p * w, w)],
            dnfull.at[1 - c, :, pl.ds(p * w, w)],
            f_send.at[p],
            f_recv.at[p],
            sibling,
        )

    per_group = max(PARTS // GROUPED, 1)
    groups = PARTS // per_group

    def g_piece(j, q):
        return gparts.at[j, :, pl.ds(q * per_group * w, per_group * w)]

    def g_copy(q, d):
        to = (chip + d) % chips
        return remote(
            g_piece(chip, q), g_piece(chip, q), g_send.at[q, d], g_recv.at[q, chip], to * 2 + c
        )

    for i in range(PARTS + 3):
        if i < PARTS:

            def other_half(s, carry, i=i):
                sib_out[i, :, pl.ds(pl.multiple_of(s * bk, bk), bk)] = product(
                    1 - c, i * sub + s
                ).astype(jnp.bfloat16)
                return carry

            def own_half(s, carry, i=i):
                acc[i, :, pl.ds(pl.multiple_of(s * bk, bk), bk)] = product(c, i * sub + s)
                return carry

            lax.fori_loop(0, sub, other_half, 0)
            sib_copy(i).start()
            lax.fori_loop(0, sub, own_half, 0)
        if 0 <= i - 1 < PARTS:
            p = i - 1
            sib_copy(p).wait_recv()
            for d in range(nz):
                at = pl.ds(pl.multiple_of((d * 2 + 1 - y) * pair, 16), pair)
                y_out[p, d] = (acc[p, at, :] + sib_in[p, at, :].astype(jnp.float32)).astype(
                    jnp.bfloat16
                )
            y_copy(p).start()
        if 0 <= i - 2 < PARTS:
            p = i - 2
            y_copy(p).wait_recv()
            for d in range(nz):
                to = along(d)
                at = pl.ds(pl.multiple_of((to * 2 + y) * pair, 16), pair)
                total = (
                    acc[p, at, :]
                    + sib_in[p, at, :].astype(jnp.float32)
                    + y_in[p, to].astype(jnp.float32)
                )
                if d == 0:
                    own[p] = total
                else:
                    z_out[p, d] = total.astype(jnp.bfloat16)
                    z_copy(p, d).start()
        if 0 <= i - 3 < PARTS:
            p = i - 3
            total = own[p]
            for d in range(1, nz):
                z_copy(p, d).wait_recv()
                total += z_in[p, d].astype(jnp.float32)
            own[p] = total
            f_copy(p).start()
            dnfull[c, :, pl.ds(p * w, w)] = own[p, pl.ds(pl.multiple_of(c * rows, 8), rows), :]
            gparts[chip, :, pl.ds(p * w, w)] = jnp.sum(
                total * xchip[:, pl.ds(p * w, w)], axis=0, keepdims=True
            )
            if (p + 1) % per_group == 0:
                q = p // per_group

                def send_g(d, carry, q=q):
                    g_copy(q, d).start()
                    return carry

                lax.fori_loop(1, chips, send_g, 0)

    for p in range(PARTS):
        f_arrival(p).wait_recv()
    mean = jnp.zeros((rows, 1), jnp.float32)
    for h in range(2):
        mean += jnp.sum(gain_ref[h] * dnfull[h] * xhat[h], axis=1, keepdims=True)
    mean = mean / (2 * half)
    for h in range(2):
        input_grad_ref[:, h * half : (h + 1) * half] = (
            scale * (gain_ref[h] * dnfull[h]) - xhat[h] * scale * mean
        ).astype(jnp.bfloat16)

    for q in range(groups):

        def wait_g(d, carry, q=q):
            j = (chip + d) % chips
            remote(
                g_piece(j, q), g_piece(j, q), g_send.at[q, d], g_recv.at[q, j], sibling
            ).wait_recv()
            return carry

        lax.fori_loop(1, chips, wait_g, 0)
    total = gparts[0]
    for j in range(1, chips):
        total += gparts[j]
    gfull[c] = total
    last = remote(gfull.at[c], gfull.at[c], h_sem.at[0], h_sem.at[1], sibling)
    last.start()
    last.wait_send()
    remote(gfull.at[1 - c], gfull.at[1 - c], h_sem.at[0], h_sem.at[1], sibling).wait_recv()
    gain_grad_ref[...] = gfull[...]

    for p in range(PARTS):
        for d in range(nz):
            to_y(p, d).wait_send()
            if d:
                to_z(p, d).wait_send()
                z_copy(p, d).wait_send()
        for j in range(chips):
            to_sibling(p, j).wait_send()
        sib_copy(p).wait_send()
        y_copy(p).wait_send()
        f_copy(p).wait_send()

    def drain_stat(d, carry):
        stat_copy(d).wait_send()
        return carry

    def drain_g(d, carry):
        for q in range(groups):
            g_copy(q, d).wait_send()
        return carry

    lax.fori_loop(1, n, drain_stat, 0)
    lax.fori_loop(1, chips, drain_g, 0)
    out_normed.wait()


def head_grad_kernel(
    dlogits_ref, normed_ref, loss_in, input_in, gain_in, out_ref, loss_ref, input_ref, gain_ref
):
    @pl.when(pl.program_id(0) == 0)
    def _():
        loss_ref[...] = loss_in[...]
        input_ref[...] = input_in[...]
        gain_ref[...] = gain_in[...]

    out_ref[...] = jnp.dot(
        dlogits_ref[...], normed_ref[...], preferred_element_type=jnp.float32
    ).astype(jnp.bfloat16)


def per_device(n, resid, gain, head, peer, labels):
    rows, depth = resid.shape
    tokens, vocab = peer.shape
    half = depth // 2
    w = half // PARTS
    bk = min(CHUNK, w)
    nk = depth // bk
    nz = n // 4
    chips = n // 2
    pair = 2 * rows
    f32, bf16 = jnp.float32, jnp.bfloat16
    dma = pltpu.SemaphoreType.DMA
    vmem = pl.BlockSpec(memory_space=pltpu.VMEM)
    hbm = pl.BlockSpec(memory_space=pl.ANY)
    loss, input_grad, gain_grad, dlogits, normed = pl.pallas_call(
        functools.partial(head_kernel, n),
        out_shape=(
            jax.ShapeDtypeStruct((1, 1), f32),
            jax.ShapeDtypeStruct((rows, depth), bf16),
            jax.ShapeDtypeStruct((2, 1, half), f32),
            jax.ShapeDtypeStruct((vocab, tokens), bf16),
            jax.ShapeDtypeStruct((2, tokens, half), bf16),
        ),
        in_specs=[vmem, vmem, hbm, vmem, vmem],
        out_specs=(vmem, vmem, vmem, vmem, hbm),
        scratch_shapes=[
            pltpu.VMEM((nk, vocab, bk), bf16),
            pltpu.VMEM((2, tokens, half), bf16),
            pltpu.VMEM((2, rows, half), f32),
            pltpu.VMEM((rows, half), f32),
            pltpu.VMEM((pair, half), f32),
            pltpu.VMEM((vocab, tokens), f32),
            pltpu.VMEM((vocab, tokens), f32),
            pltpu.VMEM((vocab, tokens), f32),
            pltpu.VMEM((vocab, tokens), f32),
            pltpu.VMEM((n, 8, tokens), f32),
            pltpu.VMEM((tokens, vocab), bf16),
            pltpu.VMEM((PARTS, tokens, w), f32),
            pltpu.VMEM((PARTS, tokens, w), bf16),
            pltpu.VMEM((PARTS, tokens, w), bf16),
            pltpu.VMEM((PARTS, nz, pair, w), bf16),
            pltpu.VMEM((PARTS, nz, pair, w), bf16),
            pltpu.VMEM((PARTS, nz, pair, w), bf16),
            pltpu.VMEM((PARTS, nz, pair, w), bf16),
            pltpu.VMEM((PARTS, pair, w), f32),
            pltpu.VMEM((2, rows, half), f32),
            pltpu.VMEM((chips, 1, half), f32),
            pltpu.VMEM((2, 1, half), f32),
            dma((nk,)),
            dma((2,)),
            dma((PARTS, nz)),
            dma((PARTS, nz)),
            dma((PARTS, chips)),
            dma((PARTS, chips)),
            dma((PARTS, chips)),
            dma((n,)),
            dma((n,)),
            dma((2, PARTS)),
            dma((2, PARTS)),
            dma((PARTS, nz)),
            dma((PARTS, nz)),
            dma((PARTS,)),
            dma((PARTS,)),
            dma((PARTS, chips)),
            dma((PARTS, chips)),
            dma((2,)),
            dma((1,)),
        ],
        compiler_params=pltpu.CompilerParams(
            collective_id=0, has_side_effects=True, vmem_limit_bytes=VMEM_BYTES
        ),
        cost_estimate=pl.CostEstimate(
            flops=4 * tokens * vocab * depth,
            bytes_accessed=2 * vocab * depth,
            transcendentals=4 * tokens * vocab,
        ),
    )(resid, gain.reshape(2, 1, half), head, peer.T, labels.reshape(1, tokens))

    wide = min(OUT_COLUMNS, half)
    per_half = half // wide
    small = [
        pl.BlockSpec((1, 1), lambda k: (0, 0)),
        pl.BlockSpec((rows, depth), lambda k: (0, 0)),
        pl.BlockSpec((2, 1, half), lambda k: (0, 0, 0)),
    ]
    head_grad, loss, input_grad, gain_grad = pl.pallas_call(
        head_grad_kernel,
        grid=(depth // wide,),
        out_shape=(
            jax.ShapeDtypeStruct((vocab, depth), bf16),
            jax.ShapeDtypeStruct((1, 1), f32),
            jax.ShapeDtypeStruct((rows, depth), bf16),
            jax.ShapeDtypeStruct((2, 1, half), f32),
        ),
        in_specs=[
            pl.BlockSpec((vocab, tokens), lambda k: (0, 0)),
            pl.BlockSpec((None, tokens, wide), lambda k: (k // per_half, 0, k % per_half)),
        ]
        + small,
        out_specs=[pl.BlockSpec((vocab, wide), lambda k: (0, k))] + small,
        compiler_params=pltpu.CompilerParams(vmem_limit_bytes=VMEM_BYTES),
        cost_estimate=pl.CostEstimate(
            flops=2 * tokens * vocab * depth,
            bytes_accessed=2 * vocab * depth,
            transcendentals=0,
        ),
    )(dlogits, normed, loss, input_grad, gain_grad)
    return loss.reshape(1), input_grad, head_grad, gain_grad.reshape(depth)


def solution(mesh):
    return jax.shard_map(
        functools.partial(per_device, mesh.shape["tensor"]),
        mesh=mesh,
        in_specs=(
            P(("groups", "tensor"), None),
            P(),
            P("tensor", None),
            P("groups", "tensor"),
            P("groups"),
        ),
        out_specs=(
            P("groups"),
            P(("groups", "tensor"), None),
            P(("groups", "tensor"), None),
            P("groups"),
        ),
        check_vma=False,
    )
```
